32 devices in a mesh: expert: 32 (over z, y, x, core), dp: 1.
Axes of the slice: x: 2, y: 2, z: 4, core: 2. Of those that a mesh axis runs over, the one named last changes fastest.
Arguments:
- tokens: bfloat16 [512, 7168], P(('dp', 'expert')), may hold values from -6 to 6
- slot_ids: int32 [512, 4], P(('dp', 'expert')), may hold values from 0 to 7, all different within a row; in each aligned block of 16 rows (0 to 15, 16 to 31, ...) at most 16 rows name the same one
- route_weights: float32 [512, 4], P(('dp', 'expert')), may hold values from 0.2 to 1
- pair_swap: int32 [4], replicated, may hold values from 0 to 1, as said below
- w_gate: bfloat16 [32, 7168, 256], P('expert'), may hold values from -0.0625 to 0.0625
- w_up: bfloat16 [32, 7168, 256], P('expert'), may hold values from -0.0625 to 0.0625
- w_down: bfloat16 [32, 256, 7168], P('expert'), may hold values from -0.1875 to 0.1875
Outputs:
- mixed: bfloat16 [512, 7168], P(('dp', 'expert'))
The draws below stay inside these ranges and needn't reach their ends.
Inputs may be any that keep to these rules, and one draw needn't show every extreme that they name: `slot_ids`: each row names 4 different slots; among the rows of one device no slot is named more than 16 times, a bound that some block reaches. `pair_swap`: some pair trades its weights and some pair does not.
All inputs are finite; a program needn't handle non-finite values.
Results may differ from the reference program's by a relative error of at most 0.0059.
Values may be sent and summed in bfloat16 or wider, within the bound.
A program may use at most 128 MiB of HBM per device.

```python
import math
import jax
import jax.numpy as jnp
import numpy as np

D = 7168
FF_WIN = 1024
SPAN = 4
ROW_DEV = 16
HID_DEV = 256
SLOTS = 8
TOP = 4
CAP = 16
ROWS = 512
N_EXPERT = 32


def draw_pair_swap(key, part):
    count = SLOTS // 2
    drawn = jax.random.randint(jax.random.fold_in(key, 17), (count,), 0, 2)
    first = jax.random.randint(jax.random.fold_in(key, 23), (), 0, count)
    offset = jax.random.randint(jax.random.fold_in(key, 29), (), 1, count)
    second = (first + offset) % count
    where_at = jnp.arange(count, dtype=jnp.int32)
    forced = jnp.where(where_at == first, 1, drawn)
    return jnp.where(where_at == second, 0, forced).astype(jnp.int32)


def levels(stream_key, extent, cuts, least, high):
    factor_of, own = 1.0, jax.random.fold_in(stream_key, 6)
    for dim, parts in cuts:
        heights = jnp.exp(jax.random.uniform(jax.random.fold_in(own, dim), (parts,), jnp.float32, least / len(cuts), high / len(cuts)))
        factor_of = factor_of * jnp.repeat(heights, extent[dim] // parts).reshape([-1 if axis == dim else 1 for axis in range(len(extent))])
    return factor_of


def shared_out(key, own, number, rows, count, top, bound, skew):
    ranking = jax.random.permutation(key, count)
    heavy_load, common = shares(count, rows * top, bound, skew, True), shares(count, rows * top, bound, skew, False)
    places = jnp.arange(count)

    def named(lengths, rotation):
        used = int((lengths > 0).sum())
        fixed = max(1, used // 4)
        passed = fixed + (places - fixed + rotation * (used - fixed)) % max(1, count - fixed)
        return jnp.zeros((count,), jnp.int32).at[ranking[jnp.where(places < fixed, places, passed)]].set(jnp.asarray(lengths, jnp.int32))

    lengths = jnp.where(number % 4 == 0, named(heavy_load, number // 4), named(common, number - number // 4 - 1))
    mixed = jax.random.permutation(jax.random.fold_in(own, 3), count)
    source_of, receiver = mixed[0:count // 2 * 2:2], mixed[1:count // 2 * 2:2]
    margin = jnp.minimum(lengths[source_of] - 1, bound - lengths[receiver]) // 2
    margin = jnp.where((source_of == ranking[0]) | (receiver == ranking[0]) | (lengths[receiver] == 0), 0, jnp.maximum(margin, 0))
    passed = jax.random.randint(jax.random.fold_in(own, 4), (count // 2,), 0, 1 << 20) % (margin + 1)
    lengths = lengths.at[source_of].add(-passed).at[receiver].add(passed)
    items = jnp.searchsorted(jnp.cumsum(lengths), jnp.arange(rows * top), side="right").astype(jnp.int32)
    grid = items.reshape(top, rows).T
    grid = grid[jax.random.permutation(jax.random.fold_in(own, 1), rows)]
    rotation = jax.random.randint(jax.random.fold_in(own, 2), (rows, 1), 0, top)
    return jnp.take_along_axis(grid, (jnp.arange(top)[None, :] + rotation) % top, axis=1)


def shares(count, total, bound, lean, full):
    portions = [(1 << 20) // math.isqrt(rank ** lean) + 1 for rank in range(1, count + 1)]
    largest = bound if full else min(bound, max(-(-total // count), total * portions[0] // sum(portions)))
    least = 1 if total - largest >= count - 1 else 0
    counts, rest = [largest] + [least] * (count - 1), total - largest - least * (count - 1)
    while rest > 0:
        candidates = [i for i in range(1, count) if counts[i] < largest] or [i for i in range(1, count) if counts[i] < bound]
        whole, budget = sum([portions[i] for i in candidates]), rest
        for i in candidates:
            addition = min(bound - counts[i], max(1, budget * portions[i] // whole), rest)
            counts[i] = counts[i] + addition
            rest = rest - addition
    return np.array(counts)


def scatter_about(stream_key, dims, width, most, split=(), held_as=jnp.bfloat16):
    loudness = levels(stream_key, dims, split, -0.22, 0.18) if split else 1.0
    values = jax.random.normal(stream_key, dims, jnp.float32) * width * loudness
    return jnp.minimum(jnp.maximum(values, -most), most).astype(held_as)


def setup_inputs(seed: int = 0, part: int = 0) -> dict:
    splits = jax.random.split(jax.random.key(seed), 8)
    part_splits = jax.random.split(jax.random.fold_in(splits[7], part), 8)
    tokens = scatter_about(part_splits[0], (ROWS, D), 1.0, 6.0, ((0, 32),))
    slot_ids_keys = jax.random.split(jax.random.fold_in(part_splits[1], 1), ROWS // ROW_DEV)
    slot_ids_turns = jax.random.permutation(jax.random.fold_in(part_splits[1], 3), ROWS // ROW_DEV)
    slot_ids = jax.vmap(lambda own, number: shared_out(jax.random.fold_in(part_splits[1], 2), own, number, ROW_DEV, SLOTS, TOP, CAP, 2))(slot_ids_keys, slot_ids_turns).reshape((ROWS, TOP))
    route_weights = jnp.clip(0.2 + 0.8 * jax.random.uniform(part_splits[2], (ROWS, TOP), jnp.float32) ** levels(part_splits[2], (ROWS, TOP), ((0, 32),), -0.2, 0.2), 0.2, 1.0)
    pair_swap = draw_pair_swap(jax.random.fold_in(splits[7], 71), part)
    w_gate = scatter_about(splits[4], (N_EXPERT, D, HID_DEV), D ** -0.5, 0.0625, ((0, 32),))
    w_up = scatter_about(splits[5], (N_EXPERT, D, HID_DEV), D ** -0.5, 0.0625, ((0, 32),))
    w_down = scatter_about(splits[6], (N_EXPERT, HID_DEV, D), FF_WIN ** -0.5, 0.1875, ((0, 32),))
    return dict(tokens=tokens, slot_ids=slot_ids, route_weights=route_weights, pair_swap=pair_swap, w_gate=w_gate, w_up=w_up, w_down=w_down)


def reference(tokens, slot_ids, route_weights, pair_swap, w_gate, w_up, w_down):
    picks = slot_ids.reshape(-1)
    pick_weights = route_weights.reshape(-1)
    owners = jnp.arange(picks.shape[0], dtype=jnp.int32) // TOP
    most_rows = N_EXPERT * CAP
    mixed = jnp.zeros(tokens.shape, jnp.float32)
    for slot in range(SLOTS):
        source = slot ^ pair_swap[slot // 2]
        order = jnp.argsort((picks != slot).astype(jnp.int32), stable=True)[:most_rows]
        valid = picks[order] == slot
        row_index = owners[order]
        rows_in = tokens[row_index]
        total = jnp.zeros((most_rows, tokens.shape[1]), jnp.float32)
        for shard in range(SPAN):
            block = shard * SLOTS + source
            gate = jnp.dot(rows_in, w_gate[block], preferred_element_type=jnp.float32)
            up = jnp.dot(rows_in, w_up[block], preferred_element_type=jnp.float32)
            hidden = (jax.nn.silu(gate) * up).astype(jnp.bfloat16)
            partial_value = jnp.dot(hidden, w_down[block], preferred_element_type=jnp.float32).astype(jnp.bfloat16)
            total = total + partial_value.astype(jnp.float32)
        scale = jnp.where(valid, pick_weights[order], jnp.float32(0.0))
        mixed = mixed.at[row_index].add(scale[:, None] * total)
    return mixed.astype(jnp.bfloat16)
```

```python
import functools
import jax
import jax.numpy as jnp
from jax import lax
from jax.experimental import pallas as pl
from jax.experimental.pallas import tpu as pltpu
from jax.sharding import PartitionSpec as P

LANES = 128
CORE, ALONG_X, ALONG_Y = 1, 2, 4
SQUARE_SLOTS = 8


def flipped(index, bit):
    return index + bit - 2 * bit * ((index // bit) % 2)


def kernel(
    span,
    pair_ref,
    ids_ref,
    route_ref,
    tokens_hbm,
    gate_hbm,
    up_hbm,
    down_hbm,
    out_ref,
    tok,
    wg,
    wu,
    wd,
    gate_acc,
    up_acc,
    hid,
    hid_out,
    own_sum,
    x_pend,
    y_pend,
    x_out,
    y_out,
    d_out,
    x_in,
    y_in,
    d_in,
    z_out,
    z_in,
    local_sem,
    send_sem,
    recv_sem,
):
    rows, width = out_ref.shape
    slots = SQUARE_SLOTS
    half = width // 2
    me = lax.axis_index("expert")
    own = me % slots
    z = me // slots
    c = me % 2
    x_peer, y_peer, core_peer = flipped(me, ALONG_X), flipped(me, ALONG_Y), flipped(me, CORE)

    def along_z(k, base):
        return ((z + k) % span) * slots + base

    partners = [along_z(k, own) for k in range(1, span)]
    partners += [along_z(k, flipped(own, CORE)) for k in range(span)]
    partners += [x_peer, y_peer]

    my_half = pl.ds(pl.multiple_of(c * half, LANES), half)
    other_half = pl.ds(pl.multiple_of((1 - c) * half, LANES), half)

    loads = [
        pltpu.make_async_copy(tokens_hbm, tok.at[0, 0, 0, :, pl.ds(0, width)], local_sem.at[0]),
        pltpu.make_async_copy(gate_hbm.at[0], wg, local_sem.at[1]),
        pltpu.make_async_copy(up_hbm.at[0], wu, local_sem.at[2]),
        pltpu.make_async_copy(down_hbm.at[0, :, my_half], wd.at[0], local_sem.at[3]),
    ]
    for load in loads:
        load.start()

    barrier = pltpu.get_barrier_semaphore()
    for partner in partners:
        pl.semaphore_signal(
            barrier, inc=1, device_id={"expert": partner}, device_id_type=pl.DeviceIdType.MESH
        )

    lane = lax.broadcasted_iota(jnp.int32, (rows, LANES), 1)
    dense = jnp.zeros((rows, LANES), jnp.float32)
    for k in range(ids_ref.shape[1]):
        dense += jnp.where(ids_ref[:, k : k + 1] == lane % slots, route_ref[:, k : k + 1], 0.0)
    first = dense.astype(jnp.bfloat16).astype(jnp.float32)
    second = (dense - first).astype(jnp.bfloat16).astype(jnp.float32)
    third = dense - first - second
    term = lane // slots
    coded = jnp.where(
        term == 0, first, jnp.where(term == 1, second, jnp.where(term == 2, third, 0.0))
    )
    tok[0, 0, 0, :, pl.ds(width, LANES)] = coded.astype(jnp.bfloat16)

    swap = pair_ref[own // 2]
    slot = own + swap * (1 - 2 * (own % 2))

    count = [0]
    sent = []

    def message(src, dst, device):
        i = count[0]
        count[0] += 1
        return pltpu.make_async_remote_copy(
            src_ref=src,
            dst_ref=dst,
            send_sem=send_sem.at[i],
            recv_sem=recv_sem.at[i],
            device_id={"expert": device},
            device_id_type=pl.DeviceIdType.MESH,
        )

    def start(copy):
        copy.start()
        sent.append(copy)

    left, right = pl.ds(0, half), pl.ds(half, half + LANES)
    by_z = {
        p: message(tok.at[0, 0, 0], tok.at[0, 0, p], along_z(span - p, own)) for p in range(1, span)
    }
    by_x = [message(tok.at[0, 0, p], tok.at[1, 0, p], x_peer) for p in range(span)]
    by_y = [message(tok.at[0, 0, p], tok.at[2, 0, p], y_peer) for p in range(span)]
    to_core = [
        [message(tok.at[g, 0, p], tok.at[g, 1, p], core_peer) for p in range(span)] for g in range(3)
    ]
    far_left = [
        message(tok.at[1, 0, p, :, left], tok.at[3, 0, p, :, left], y_peer) for p in range(span)
    ]
    far_right = [
        message(tok.at[2, 0, p, :, right], tok.at[3, 0, p, :, right], x_peer) for p in range(span)
    ]
    core_left = [
        message(tok.at[3, 0, p, :, left], tok.at[3, 1, p, :, left], core_peer) for p in range(span)
    ]
    core_right = [
        message(tok.at[3, 0, p, :, right], tok.at[3, 1, p, :, right], core_peer)
        for p in range(span)
    ]
    swap_down = message(down_hbm.at[0, :, other_half], wd.at[1], core_peer)
    swap_hidden = [message(hid_out.at[g], hid.at[g, 1], core_peer) for g in range(4)]
    x_early = message(x_out.at[0], x_in.at[0], x_peer)
    y_early = message(y_out.at[1], y_in.at[1], y_peer)
    d_to_x = [message(d_out.at[0, p], d_in.at[0, p], x_peer) for p in range(span)]
    d_to_y = [message(d_out.at[1, p], d_in.at[1, p], y_peer) for p in range(span)]
    x_late = [message(x_out.at[1, p], x_in.at[1, p], x_peer) for p in range(span)]
    y_late = [message(y_out.at[0, p], y_in.at[0, p], y_peer) for p in range(span)]
    home = {
        (r, p): message(
            z_out.at[r, p],
            z_in.at[r, (span - p) % span],
            along_z(p, own if r == 0 else flipped(own, CORE)),
        )
        for r in range(2)
        for p in range(span)
        if (r, p) != (0, 0)
    }

    def project(g):
        depth = 1024 if width % 1024 == 0 else width
        gate_acc[...] = jnp.zeros_like(gate_acc)
        up_acc[...] = jnp.zeros_like(up_acc)

        def step(i, _):
            part = pl.ds(pl.multiple_of(i * depth, LANES), depth)
            x = tok[g, :, :, :, part].reshape(2 * span * rows, depth)
            gate_acc[...] += jnp.dot(x, wg[part, :], preferred_element_type=jnp.float32)
            up_acc[...] += jnp.dot(x, wu[part, :], preferred_element_type=jnp.float32)
            return 0

        lax.fori_loop(0, width // depth, step, 0)
        code = tok[g, :, :, :, pl.ds(width, LANES)].reshape(2 * span * rows, LANES)
        lanes = lax.broadcasted_iota(jnp.int32, code.shape, 1)
        weight = jnp.sum(
            jnp.where(lanes % slots == slot, code.astype(jnp.float32), 0.0), 1, keepdims=True
        )
        gate = gate_acc[...]
        value = (gate / (1.0 + jnp.exp(-gate)) * up_acc[...] * weight).astype(jnp.bfloat16)
        many = span * rows
        hid[g, 0] = value
        hid_out[g, pl.ds(0, many)] = value[many:]
        hid_out[g, pl.ds(many, many)] = value[:many]
        start(swap_hidden[g])

    def expand(g, first_to, second_to):
        wide = 512 if half % 512 == 0 else half
        many = span * rows
        swap_hidden[g].wait_recv()

        def step(i, _):
            part = pl.ds(pl.multiple_of(i * wide, LANES), wide)
            total = jnp.dot(hid[g, 0], wd[0, :, part], preferred_element_type=jnp.float32)
            total += jnp.dot(hid[g, 1], wd[1, :, part], preferred_element_type=jnp.float32)
            for ref, piece in ((first_to, total[:many]), (second_to, total[many:])):
                ref[:, :, part] = piece.reshape(span, rows, wide).astype(ref.dtype)
            return 0

        lax.fori_loop(0, half // wide, step, 0)

    def gathered(p):
        if p:
            by_z[p].wait_recv()
        start(by_x[p])
        start(by_y[p])
        start(to_core[0][p])

    def crossed(p):
        by_x[p].wait_recv()
        start(far_left[p])
        start(to_core[1][p])
        by_y[p].wait_recv()
        start(far_right[p])
        start(to_core[2][p])

    def cornered(p):
        far_left[p].wait_recv()
        start(core_left[p])
        far_right[p].wait_recv()
        start(core_right[p])

    loads[0].wait()
    pl.semaphore_wait(barrier, len(partners))
    for p in range(1, span):
        start(by_z[p])
    gathered(0)
    start(swap_down)
    order = [p for p in (1, span - 1) if p < span] + list(range(2, span - 1))
    done = [0]
    for p in order:
        gathered(p)
        crossed(done[-1])
        if len(done) > 1:
            cornered(done[-2])
        done.append(p)
    for load in loads[1:3]:
        load.wait()
    for p in range(span):
        to_core[0][p].wait_recv()
    project(0)
    crossed(done[-1])
    cornered(done[-2])
    for p in range(span):
        to_core[1][p].wait_recv()
    project(1)
    cornered(done[-1])
    for p in range(span):
        to_core[2][p].wait_recv()
    project(2)
    loads[3].wait()
    swap_down.wait_recv()
    expand(1, x_out.at[0], x_pend)
    start(x_early)
    expand(2, y_pend, y_out.at[1])
    start(y_early)
    for p in range(span):
        core_left[p].wait_recv()
        core_right[p].wait_recv()
    project(3)
    expand(0, own_sum.at[0], own_sum.at[1])
    expand(3, d_out.at[0], d_out.at[1])
    order = order + [0]
    for p in order:
        start(d_to_x[p])
        start(d_to_y[p])
    for p in order:
        d_to_y[p].wait_recv()
        x_out[1, p] = (x_pend[p] + d_in[1, p].astype(jnp.float32)).astype(jnp.bfloat16)
        start(x_late[p])
        d_to_x[p].wait_recv()
        y_out[0, p] = (y_pend[p] + d_in[0, p].astype(jnp.float32)).astype(jnp.bfloat16)
        start(y_late[p])
    x_early.wait_recv()
    y_early.wait_recv()
    for p in order:
        x_late[p].wait_recv()
        y_late[p].wait_recv()
        for r in range(2):
            total = own_sum[r, p] + x_in[r, p].astype(jnp.float32) + y_in[r, p].astype(jnp.float32)
            if (r, p) == (0, 0):
                own_sum[r, p] = total
            else:
                z_out[r, p] = total.astype(jnp.bfloat16)
                start(home[r, p])
    for copy in home.values():
        copy.wait_recv()
    total = own_sum[0, 0]
    for p in range(1, span):
        total += z_in[0, p].astype(jnp.float32)
    out_ref[:, my_half] = total.astype(jnp.bfloat16)
    total = z_in[1, 0].astype(jnp.float32)
    for p in range(1, span):
        total += z_in[1, p].astype(jnp.float32)
    out_ref[:, other_half] = total.astype(jnp.bfloat16)
    for copy in sent:
        copy.wait_send()


def squares(tokens, slot_ids, route_weights, pair_swap, w_gate, w_up, w_down):
    span = lax.axis_size("expert") // SQUARE_SLOTS
    rows, width = tokens.shape
    hidden = w_gate.shape[2]
    half = width // 2
    wide = width + LANES
    group = 2 * span * rows
    messages = (span - 1) + 9 * span + 1 + 4 + 2 + 4 * span + 2 * span - 1
    bf16, f32 = jnp.bfloat16, jnp.float32
    column = (span, rows, half)
    vmem = pl.BlockSpec(memory_space=pltpu.VMEM)
    hbm = pl.BlockSpec(memory_space=pl.ANY)
    return pl.pallas_call(
        functools.partial(kernel, span),
        out_shape=jax.ShapeDtypeStruct((rows, width), bf16),
        in_specs=[pl.BlockSpec(memory_space=pltpu.SMEM), vmem, vmem, hbm, hbm, hbm, hbm],
        out_specs=vmem,
        scratch_shapes=[
            pltpu.VMEM((4, 2, span, rows, wide), bf16),
            pltpu.VMEM((width, hidden), bf16),
            pltpu.VMEM((width, hidden), bf16),
            pltpu.VMEM((2, hidden, half), bf16),
            pltpu.VMEM((group, hidden), f32),
            pltpu.VMEM((group, hidden), f32),
            pltpu.VMEM((4, 2, group, hidden), bf16),
            pltpu.VMEM((4, group, hidden), bf16),
            pltpu.VMEM((2,) + column, f32),
            pltpu.VMEM(column, f32),
            pltpu.VMEM(column, f32),
        ]
        + [pltpu.VMEM((2,) + column, bf16)] * 8
        + [
            pltpu.SemaphoreType.DMA((4,)),
            pltpu.SemaphoreType.DMA((messages,)),
            pltpu.SemaphoreType.DMA((messages,)),
        ],
        compiler_params=pltpu.CompilerParams(
            collective_id=0, has_side_effects=True, vmem_limit_bytes=56 * 2**20
        ),
    )(pair_swap, slot_ids, route_weights, tokens, w_gate, w_up, w_down)


def whole(tokens, slot_ids, route_weights, pair_swap, w_gate, w_up, w_down):
    slots = 2 * pair_swap.shape[0]
    own = lax.axis_index("expert") % slots
    pair = jnp.arange(pair_swap.shape[0], dtype=jnp.int32)
    swap = jnp.sum(jnp.where(pair == own // 2, pair_swap, 0))
    slot = own + swap * (1 - 2 * (own % 2))
    named = slot_ids[:, :, None] == jnp.arange(slots, dtype=jnp.int32)
    dense = jnp.sum(jnp.where(named, route_weights[:, :, None], 0.0), 1)
    rows = lax.all_gather(tokens, "expert", axis=0, tiled=True)
    dense = lax.all_gather(dense, "expert", axis=0, tiled=True)
    mine = jnp.arange(slots, dtype=jnp.int32) == slot
    weight = jnp.sum(jnp.where(mine, dense, 0.0), 1, keepdims=True)
    gate = jnp.dot(rows, w_gate[0], preferred_element_type=jnp.float32)
    up = jnp.dot(rows, w_up[0], preferred_element_type=jnp.float32)
    hidden = (jax.nn.silu(gate) * up).astype(jnp.bfloat16)
    value = jnp.dot(hidden, w_down[0], preferred_element_type=jnp.float32) * weight
    mixed = lax.psum_scatter(value, "expert", scatter_dimension=0, tiled=True)
    return mixed.astype(jnp.bfloat16)


def on_device(*args):
    slots = 2 * args[3].shape[0]
    return (squares if slots == SQUARE_SLOTS else whole)(*args)


def solution(mesh):
    return jax.shard_map(
        on_device,
        mesh=mesh,
        in_specs=(
            P(("dp", "expert"), None),
            P(("dp", "expert"), None),
            P(("dp", "expert"), None),
            P(),
            P("expert", None, None),
            P("expert", None, None),
            P("expert", None, None),
        ),
        out_specs=P(("dp", "expert"), None),
        check_vma=False,
    )
```

```python
import functools
import jax
import jax.numpy as jnp
from jax import lax
from jax.experimental import pallas as pl
from jax.experimental.pallas import tpu as pltpu
from jax.sharding import PartitionSpec as P

LANES = 128
CORE, ALONG_X, ALONG_Y = 1, 2, 4
SQUARE_SLOTS = 8
COLUMN = 4


def flipped(index, bit):
    return index + bit - 2 * bit * ((index // bit) % 2)


def kernel(
    span,
    pair_ref,
    ids_ref,
    route_ref,
    tokens_hbm,
    gate_hbm,
    up_hbm,
    down_hbm,
    out_ref,
    tok,
    wg,
    wu,
    wd,
    gate_acc,
    up_acc,
    hid,
    hid_out,
    own_sum,
    x_pend,
    y_pend,
    x_out,
    y_out,
    d_out,
    x_in,
    y_in,
    d_in,
    z_out,
    z_in,
    local_sem,
    send_sem,
    recv_sem,
    chain_send,
    chain_recv,
):
    rows, width = out_ref.shape
    slots = SQUARE_SLOTS
    half = width // 2
    me = lax.axis_index("expert")
    own = me % slots
    z = me // slots
    c = me % 2
    x_peer, y_peer, core_peer = flipped(me, ALONG_X), flipped(me, ALONG_Y), flipped(me, CORE)

    def along_z(k, base):
        return ((z + k) % span) * slots + base

    partners = [along_z(k, own) for k in range(1, span)]
    partners += [along_z(k, flipped(own, CORE)) for k in range(span)]
    partners += [x_peer, y_peer]

    my_half = pl.ds(pl.multiple_of(c * half, LANES), half)
    other_half = pl.ds(pl.multiple_of((1 - c) * half, LANES), half)

    loads = [
        pltpu.make_async_copy(tokens_hbm, tok.at[0, 0, z, :, pl.ds(0, width)], local_sem.at[0]),
        pltpu.make_async_copy(gate_hbm.at[0], wg, local_sem.at[1]),
        pltpu.make_async_copy(up_hbm.at[0], wu, local_sem.at[2]),
        pltpu.make_async_copy(down_hbm.at[0, :, my_half], wd.at[0], local_sem.at[3]),
    ]
    for load in loads:
        load.start()

    barrier = pltpu.get_barrier_semaphore()
    for partner in partners:
        pl.semaphore_signal(
            barrier, inc=1, device_id={"expert": partner}, device_id_type=pl.DeviceIdType.MESH
        )

    line = lax.broadcasted_iota(jnp.int32, (LANES, rows), 0)
    dense = jnp.zeros((LANES, rows), jnp.float32)
    for k in range(ids_ref.shape[0]):
        dense += jnp.where(ids_ref[k : k + 1, :] == line % slots, route_ref[k : k + 1, :], 0.0)
    first = dense.astype(jnp.bfloat16).astype(jnp.float32)
    second = (dense - first).astype(jnp.bfloat16).astype(jnp.float32)
    third = dense - first - second
    term = line // slots
    coded = jnp.where(
        term == 0, first, jnp.where(term == 1, second, jnp.where(term == 2, third, 0.0))
    )
    same = lax.broadcasted_iota(jnp.int32, (rows, rows), 0) == lax.broadcasted_iota(
        jnp.int32, (rows, rows), 1
    )
    turned = lax.dot_general(
        jnp.where(same, 1.0, 0.0).astype(jnp.bfloat16),
        coded.astype(jnp.bfloat16),
        (((1,), (1,)), ((), ())),
        preferred_element_type=jnp.float32,
    )
    tok[0, 0, z, :, pl.ds(width, LANES)] = turned.astype(jnp.bfloat16)

    swap = pair_ref[own // 2]
    slot = own + swap * (1 - 2 * (own % 2))

    count = [0]
    sent = []

    def family(size, route):
        base = count[0]
        count[0] += size

        def member(i, number=None):
            at = base + (i if number is None else number)
            src, dst, device = route(i)
            return pltpu.make_async_remote_copy(
                src_ref=src,
                dst_ref=dst,
                send_sem=send_sem.at[at],
                recv_sem=recv_sem.at[at],
                device_id={"expert": device},
                device_id_type=pl.DeviceIdType.MESH,
            )

        return member

    def start(copy):
        copy.start()
        sent.append(copy)

    left, right = pl.ds(0, half), pl.ds(half, half + LANES)
    upper = jnp.minimum(z + 1, span - 1) * slots + own
    lower = jnp.maximum(z - 1, 0) * slots + own

    def row_copy(i, device, spare):
        return pltpu.make_async_remote_copy(
            src_ref=tok.at[0, 0, i],
            dst_ref=tok.at[0, 0, i],
            send_sem=chain_send.at[spare],
            recv_sem=chain_recv.at[i],
            device_id={"expert": device},
            device_id_type=pl.DeviceIdType.MESH,
        )

    by_x = family(span, lambda i: (tok.at[0, 0, i], tok.at[1, 0, i], x_peer))
    by_y = family(span, lambda i: (tok.at[0, 0, i], tok.at[2, 0, i], y_peer))
    to_core = [
        family(span, lambda i, g=g: (tok.at[g, 0, i], tok.at[g, 1, i], core_peer)) for g in range(3)
    ]
    far_left = family(
        span, lambda i: (tok.at[1, 0, i, :, left], tok.at[3, 0, i, :, left], y_peer)
    )
    far_right = family(
        span, lambda i: (tok.at[2, 0, i, :, right], tok.at[3, 0, i, :, right], x_peer)
    )
    core_left = family(
        span, lambda i: (tok.at[3, 0, i, :, left], tok.at[3, 1, i, :, left], core_peer)
    )
    core_right = family(
        span, lambda i: (tok.at[3, 0, i, :, right], tok.at[3, 1, i, :, right], core_peer)
    )
    swap_down = family(1, lambda i: (down_hbm.at[0, :, other_half], wd.at[1], core_peer))(0)
    hidden_family = family(4, lambda g: (hid_out.at[g], hid.at[g, 1], core_peer))
    swap_hidden = [hidden_family(g) for g in range(4)]
    x_early = family(span, lambda i: (x_out.at[0, i], x_in.at[0, i], x_peer))
    y_early = family(span, lambda i: (y_out.at[1, i], y_in.at[1, i], y_peer))
    d_to_x = family(span, lambda i: (d_out.at[0, i], d_in.at[0, i], x_peer))
    d_to_y = family(span, lambda i: (d_out.at[1, i], d_in.at[1, i], y_peer))
    x_late = family(span, lambda i: (x_out.at[1, i], x_in.at[1, i], x_peer))
    y_late = family(span, lambda i: (y_out.at[0, i], y_in.at[0, i], y_peer))
    home_family = family(
        2 * span,
        lambda rp: (
            z_out.at[rp[0], rp[1]],
            z_in.at[rp[0], (span - rp[1]) % span],
            along_z(rp[1], own if rp[0] == 0 else flipped(own, CORE)),
        ),
    )
    home = {
        (r, p): home_family((r, p), r * span + p)
        for r in range(2)
        for p in range(span)
        if (r, p) != (0, 0)
    }

    def project(g):
        depth = 1024 if width % 1024 == 0 else width
        gate_acc[...] = jnp.zeros_like(gate_acc)
        up_acc[...] = jnp.zeros_like(up_acc)

        def step(i, _):
            part = pl.ds(pl.multiple_of(i * depth, LANES), depth)
            x = tok[g, :, :, :, part].reshape(2 * span * rows, depth)
            gate_acc[...] += jnp.dot(x, wg[part, :], preferred_element_type=jnp.float32)
            up_acc[...] += jnp.dot(x, wu[part, :], preferred_element_type=jnp.float32)
            return 0

        lax.fori_loop(0, width // depth, step, 0)
        code = tok[g, :, :, :, pl.ds(width, LANES)].reshape(2 * span * rows, LANES)
        lanes = lax.broadcasted_iota(jnp.int32, code.shape, 1)
        weight = jnp.sum(
            jnp.where(lanes % slots == slot, code.astype(jnp.float32), 0.0), 1, keepdims=True
        )
        gate = gate_acc[...]
        value = (gate / (1.0 + jnp.exp(-gate)) * up_acc[...] * weight).astype(jnp.bfloat16)
        many = span * rows
        hid[g, 0] = value
        hid_out[g, pl.ds(0, many)] = value[many:]
        hid_out[g, pl.ds(many, many)] = value[:many]
        start(swap_hidden[g])

    def expand(g, first_to, second_to):
        wide = 512 if half % 512 == 0 else half
        many = span * rows
        swap_hidden[g].wait_recv()

        def step(i, _):
            part = pl.ds(pl.multiple_of(i * wide, LANES), wide)
            total = jnp.dot(hid[g, 0], wd[0, :, part], preferred_element_type=jnp.float32)
            total += jnp.dot(hid[g, 1], wd[1, :, part], preferred_element_type=jnp.float32)
            for ref, piece in ((first_to, total[:many]), (second_to, total[many:])):
                ref[:, :, part] = piece.reshape(span, rows, wide).astype(ref.dtype)
            return 0

        lax.fori_loop(0, half // wide, step, 0)

    low = z < span // 2
    arrivals = [flipped(z, 1), jnp.where(low, 2, 1), jnp.where(low, 3, 0)]
    inner = (z > 0) & (z < span - 1)

    def passed_on(j):
        i = arrivals[j]
        return row_copy(i, jnp.where(i < z, upper, lower), 2 + j)

    def gathered(i):
        start(by_x(i))
        start(by_y(i))
        start(to_core[0](i))

    def crossed(i):
        by_x(i).wait_recv()
        start(far_left(i))
        start(to_core[1](i))
        by_y(i).wait_recv()
        start(far_right(i))
        start(to_core[2](i))

    def cornered(i):
        far_left(i).wait_recv()
        start(core_left(i))
        far_right(i).wait_recv()
        start(core_right(i))

    loads[0].wait()
    pl.semaphore_wait(barrier, len(partners))
    pl.when(z < span - 1)(lambda: row_copy(z, upper, 0).start())
    pl.when(z > 0)(lambda: row_copy(z, lower, 1).start())
    gathered(z)
    start(swap_down)
    done = [z]
    for j, i in enumerate(arrivals):
        row_copy(i, upper, 2 + j).wait_recv()
        pl.when(inner)(lambda j=j: passed_on(j).start())
        gathered(i)
        crossed(done[-1])
        if len(done) > 1:
            cornered(done[-2])
        done.append(i)
    for load in loads[1:3]:
        load.wait()
    for i in range(span):
        to_core[0](i).wait_recv()
    project(0)
    crossed(done[-1])
    cornered(done[-2])
    for i in range(span):
        to_core[1](i).wait_recv()
    project(1)
    cornered(done[-1])
    for i in range(span):
        to_core[2](i).wait_recv()
    project(2)
    loads[3].wait()
    swap_down.wait_recv()
    expand(1, x_out.at[0], x_pend)
    expand(2, y_pend, y_out.at[1])
    order = [(p, (z + p) % span) for p in (2, 3, 1, 0)]
    ahead = 2
    for _, i in order[:ahead]:
        start(x_early(i))
        start(y_early(i))
    for i in range(span):
        core_left(i).wait_recv()
        core_right(i).wait_recv()
    project(3)
    expand(0, own_sum.at[0], own_sum.at[1])
    expand(3, d_out.at[0], d_out.at[1])
    for _, i in order[:ahead]:
        start(d_to_x(i))
        start(d_to_y(i))

    def finish(p, i):
        for copy in (x_early(i), y_early(i), x_late(i), y_late(i)):
            copy.wait_recv()
        for r in range(2):
            total = own_sum[r, i] + x_in[r, i].astype(jnp.float32) + y_in[r, i].astype(jnp.float32)
            if (r, p) == (0, 0):
                own_sum[r, i] = total
            else:
                z_out[r, p] = total.astype(jnp.bfloat16)
                start(home[r, p])

    for n, (p, i) in enumerate(order):
        d_to_y(i).wait_recv()
        x_out[1, i] = (x_pend[i] + d_in[1, i].astype(jnp.float32)).astype(jnp.bfloat16)
        start(x_late(i))
        d_to_x(i).wait_recv()
        y_out[0, i] = (y_pend[i] + d_in[0, i].astype(jnp.float32)).astype(jnp.bfloat16)
        start(y_late(i))
        if n + ahead < span:
            start(x_early(order[n + ahead][1]))
            start(y_early(order[n + ahead][1]))
            start(d_to_x(order[n + ahead][1]))
            start(d_to_y(order[n + ahead][1]))
        if n:
            finish(*order[n - 1])
    finish(*order[-1])
    for copy in home.values():
        copy.wait_recv()
    total = own_sum[0, z]
    for p in range(1, span):
        total += z_in[0, p].astype(jnp.float32)
    out_ref[:, my_half] = total.astype(jnp.bfloat16)
    total = z_in[1, 0].astype(jnp.float32)
    for p in range(1, span):
        total += z_in[1, p].astype(jnp.float32)
    out_ref[:, other_half] = total.astype(jnp.bfloat16)
    for copy in sent:
        copy.wait_send()
    pl.when(z < span - 1)(lambda: row_copy(z, upper, 0).wait_send())
    pl.when(z > 0)(lambda: row_copy(z, lower, 1).wait_send())
    for j in range(span - 1):
        pl.when(inner)(lambda j=j: passed_on(j).wait_send())


def squares(tokens, slot_ids, route_weights, pair_swap, w_gate, w_up, w_down):
    span = lax.axis_size("expert") // SQUARE_SLOTS
    rows, width = tokens.shape
    hidden = w_gate.shape[2]
    half = width // 2
    wide = width + LANES
    group = 2 * span * rows
    messages = 9 * span + 1 + 4 + 6 * span + 2 * span + 4 + span
    bf16, f32 = jnp.bfloat16, jnp.float32
    column = (span, rows, half)
    vmem = pl.BlockSpec(memory_space=pltpu.VMEM)
    hbm = pl.BlockSpec(memory_space=pl.ANY)
    return pl.pallas_call(
        functools.partial(kernel, span),
        out_shape=jax.ShapeDtypeStruct((rows, width), bf16),
        in_specs=[pl.BlockSpec(memory_space=pltpu.SMEM), vmem, vmem, hbm, hbm, hbm, hbm],
        out_specs=vmem,
        scratch_shapes=[
            pltpu.VMEM((4, 2, span, rows, wide), bf16),
            pltpu.VMEM((width, hidden), bf16),
            pltpu.VMEM((width, hidden), bf16),
            pltpu.VMEM((2, hidden, half), bf16),
            pltpu.VMEM((group, hidden), f32),
            pltpu.VMEM((group, hidden), f32),
            pltpu.VMEM((4, 2, group, hidden), bf16),
            pltpu.VMEM((4, group, hidden), bf16),
            pltpu.VMEM((2,) + column, f32),
            pltpu.VMEM(column, f32),
            pltpu.VMEM(column, f32),
        ]
        + [pltpu.VMEM((2,) + column, bf16)] * 8
        + [
            pltpu.SemaphoreType.DMA((4,)),
            pltpu.SemaphoreType.DMA((messages,)),
            pltpu.SemaphoreType.DMA((messages,)),
            pltpu.SemaphoreType.DMA((span + 1,)),
            pltpu.SemaphoreType.DMA((span,)),
        ],
        compiler_params=pltpu.CompilerParams(
            collective_id=0, has_side_effects=True, vmem_limit_bytes=56 * 2**20
        ),
    )(pair_swap, slot_ids.T, route_weights.T, tokens, w_gate, w_up, w_down)


def whole(tokens, slot_ids, route_weights, pair_swap, w_gate, w_up, w_down):
    slots = 2 * pair_swap.shape[0]
    own = lax.axis_index("expert") % slots
    pair = jnp.arange(pair_swap.shape[0], dtype=jnp.int32)
    swap = jnp.sum(jnp.where(pair == own // 2, pair_swap, 0))
    slot = own + swap * (1 - 2 * (own % 2))
    named = slot_ids[:, :, None] == jnp.arange(slots, dtype=jnp.int32)
    dense = jnp.sum(jnp.where(named, route_weights[:, :, None], 0.0), 1)
    rows = lax.all_gather(tokens, "expert", axis=0, tiled=True)
    dense = lax.all_gather(dense, "expert", axis=0, tiled=True)
    mine = jnp.arange(slots, dtype=jnp.int32) == slot
    weight = jnp.sum(jnp.where(mine, dense, 0.0), 1, keepdims=True)
    gate = jnp.dot(rows, w_gate[0], preferred_element_type=jnp.float32)
    up = jnp.dot(rows, w_up[0], preferred_element_type=jnp.float32)
    hidden = (jax.nn.silu(gate) * up).astype(jnp.bfloat16)
    value = jnp.dot(hidden, w_down[0], preferred_element_type=jnp.float32) * weight
    mixed = lax.psum_scatter(value, "expert", scatter_dimension=0, tiled=True)
    return mixed.astype(jnp.bfloat16)


def on_device(*args):
    slots = 2 * args[3].shape[0]
    square = slots == SQUARE_SLOTS and lax.axis_size("expert") == SQUARE_SLOTS * COLUMN
    return (squares if square else whole)(*args)


def solution(mesh):
    return jax.shard_map(
        on_device,
        mesh=mesh,
        in_specs=(
            P(("dp", "expert"), None),
            P(("dp", "expert"), None),
            P(("dp", "expert"), None),
            P(),
            P("expert", None, None),
            P("expert", None, None),
            P("expert", None, None),
        ),
        out_specs=P(("dp", "expert"), None),
        check_vma=False,
    )
```

```python
import functools
import jax
import jax.numpy as jnp
from jax import lax
from jax.experimental import pallas as pl
from jax.experimental.pallas import tpu as pltpu
from jax.sharding import PartitionSpec as P

LANES = 128
CORE, ALONG_X, ALONG_Y = 1, 2, 4
SQUARE_SLOTS = 8
COLUMN = 4


def flipped(index, bit):
    return index + bit - 2 * bit * ((index // bit) % 2)


def kernel(
    span,
    pair_ref,
    ids_ref,
    route_ref,
    tokens_hbm,
    gate_hbm,
    up_hbm,
    down_hbm,
    out_ref,
    tok,
    wg,
    wu,
    wd,
    gate_acc,
    up_acc,
    hid,
    hid_out,
    own_sum,
    x_pend,
    y_pend,
    x_out,
    y_out,
    d_out,
    x_in,
    y_in,
    d_in,
    z_out,
    z_in,
    local_sem,
    send_sem,
    recv_sem,
    chain_send,
    chain_recv,
):
    rows, width = out_ref.shape
    slots = SQUARE_SLOTS
    half = width // 2
    me = lax.axis_index("expert")
    own = me % slots
    z = me // slots
    c = me % 2
    x_peer, y_peer, core_peer = flipped(me, ALONG_X), flipped(me, ALONG_Y), flipped(me, CORE)

    def along_z(k, base):
        return ((z + k) % span) * slots + base

    partners = [along_z(k, own) for k in range(1, span)]
    partners += [along_z(k, flipped(own, CORE)) for k in range(span)]
    partners += [x_peer, y_peer]

    my_half = pl.ds(pl.multiple_of(c * half, LANES), half)
    other_half = pl.ds(pl.multiple_of((1 - c) * half, LANES), half)

    loads = [
        pltpu.make_async_copy(tokens_hbm, tok.at[0, 0, z, :, pl.ds(0, width)], local_sem.at[0]),
        pltpu.make_async_copy(gate_hbm.at[0], wg, local_sem.at[1]),
        pltpu.make_async_copy(up_hbm.at[0], wu, local_sem.at[2]),
        pltpu.make_async_copy(down_hbm.at[0, :, my_half], wd.at[0], local_sem.at[3]),
    ]
    for load in loads:
        load.start()

    barrier = pltpu.get_barrier_semaphore()
    for partner in partners:
        pl.semaphore_signal(
            barrier, inc=1, device_id={"expert": partner}, device_id_type=pl.DeviceIdType.MESH
        )

    line = lax.broadcasted_iota(jnp.int32, (LANES, rows), 0)
    dense = jnp.zeros((LANES, rows), jnp.float32)
    for k in range(ids_ref.shape[0]):
        dense += jnp.where(ids_ref[k : k + 1, :] == line % slots, route_ref[k : k + 1, :], 0.0)
    first = dense.astype(jnp.bfloat16).astype(jnp.float32)
    second = (dense - first).astype(jnp.bfloat16).astype(jnp.float32)
    third = dense - first - second
    term = line // slots
    coded = jnp.where(
        term == 0, first, jnp.where(term == 1, second, jnp.where(term == 2, third, 0.0))
    )
    same = lax.broadcasted_iota(jnp.int32, (rows, rows), 0) == lax.broadcasted_iota(
        jnp.int32, (rows, rows), 1
    )
    turned = lax.dot_general(
        jnp.where(same, 1.0, 0.0).astype(jnp.bfloat16),
        coded.astype(jnp.bfloat16),
        (((1,), (1,)), ((), ())),
        preferred_element_type=jnp.float32,
    )
    tok[0, 0, z, :, pl.ds(width, LANES)] = turned.astype(jnp.bfloat16)

    swap = pair_ref[own // 2]
    slot = own + swap * (1 - 2 * (own % 2))

    count = [0]
    sent = []

    def family(size, route):
        base = count[0]
        count[0] += size

        def member(i, number=None):
            at = base + (i if number is None else number)
            src, dst, device = route(i)
            return pltpu.make_async_remote_copy(
                src_ref=src,
                dst_ref=dst,
                send_sem=send_sem.at[at],
                recv_sem=recv_sem.at[at],
                device_id={"expert": device},
                device_id_type=pl.DeviceIdType.MESH,
            )

        return member

    def start(copy):
        copy.start()
        sent.append(copy)

    left, right = pl.ds(0, half), pl.ds(half, half + LANES)
    upper = jnp.minimum(z + 1, span - 1) * slots + own
    lower = jnp.maximum(z - 1, 0) * slots + own

    def row_copy(i, device, spare):
        return pltpu.make_async_remote_copy(
            src_ref=tok.at[0, 0, i],
            dst_ref=tok.at[0, 0, i],
            send_sem=chain_send.at[spare],
            recv_sem=chain_recv.at[i],
            device_id={"expert": device},
            device_id_type=pl.DeviceIdType.MESH,
        )

    by_x = family(span, lambda i: (tok.at[0, 0, i], tok.at[1, 0, i], x_peer))
    by_y = family(span, lambda i: (tok.at[0, 0, i], tok.at[2, 0, i], y_peer))
    to_core = [
        family(span, lambda i, g=g: (tok.at[g, 0, i], tok.at[g, 1, i], core_peer)) for g in range(3)
    ]
    far_left = family(
        span, lambda i: (tok.at[1, 0, i, :, left], tok.at[3, 0, i, :, left], y_peer)
    )
    far_right = family(
        span, lambda i: (tok.at[2, 0, i, :, right], tok.at[3, 0, i, :, right], x_peer)
    )
    core_left = family(
        span, lambda i: (tok.at[3, 0, i, :, left], tok.at[3, 1, i, :, left], core_peer)
    )
    core_right = family(
        span, lambda i: (tok.at[3, 0, i, :, right], tok.at[3, 1, i, :, right], core_peer)
    )
    swap_down = family(1, lambda i: (down_hbm.at[0, :, other_half], wd.at[1], core_peer))(0)
    hidden_family = family(4, lambda g: (hid_out.at[g], hid.at[g, 1], core_peer))
    swap_hidden = [hidden_family(g) for g in range(4)]
    x_early = family(span, lambda i: (x_out.at[0, i], x_in.at[0, i], x_peer))
    y_early = family(span, lambda i: (y_out.at[1, i], y_in.at[1, i], y_peer))
    d_to_x = family(span, lambda i: (d_out.at[0, i], d_in.at[0, i], x_peer))
    d_to_y = family(span, lambda i: (d_out.at[1, i], d_in.at[1, i], y_peer))
    x_late = family(span, lambda i: (x_out.at[1, i], x_in.at[1, i], x_peer))
    y_late = family(span, lambda i: (y_out.at[0, i], y_in.at[0, i], y_peer))
    home_family = family(
        2 * span,
        lambda rp: (
            z_out.at[rp[0], rp[1]],
            z_in.at[rp[0], (span - rp[1]) % span],
            along_z(rp[1], own if rp[0] == 0 else flipped(own, CORE)),
        ),
    )
    home = {
        (r, p): home_family((r, p), r * span + p)
        for r in range(2)
        for p in range(span)
        if (r, p) != (0, 0)
    }

    def project(g):
        depth = 1792 if width % 1792 == 0 else width
        gate_acc[...] = jnp.zeros_like(gate_acc)
        up_acc[...] = jnp.zeros_like(up_acc)

        def step(i, _):
            part = pl.ds(pl.multiple_of(i * depth, LANES), depth)
            x = tok[g, :, :, :, part].reshape(2 * span * rows, depth)
            gate_acc[...] += jnp.dot(x, wg[part, :], preferred_element_type=jnp.float32)
            up_acc[...] += jnp.dot(x, wu[part, :], preferred_element_type=jnp.float32)
            return 0

        lax.fori_loop(0, width // depth, step, 0)
        code = tok[g, :, :, :, pl.ds(width, LANES)].reshape(2 * span * rows, LANES)
        lanes = lax.broadcasted_iota(jnp.int32, code.shape, 1)
        weight = jnp.sum(
            jnp.where(lanes % slots == slot, code.astype(jnp.float32), 0.0), 1, keepdims=True
        )
        gate = gate_acc[...]
        value = (gate / (1.0 + jnp.exp(-gate)) * up_acc[...] * weight).astype(jnp.bfloat16)
        many = span * rows
        hid[g, 0] = value
        hid_out[g, pl.ds(0, many)] = value[many:]
        hid_out[g, pl.ds(many, many)] = value[:many]
        start(swap_hidden[g])

    def expand(g, first_to, second_to):
        wide = 1792 if half % 1792 == 0 else half
        many = span * rows
        swap_hidden[g].wait_recv()

        def step(i, _):
            part = pl.ds(pl.multiple_of(i * wide, LANES), wide)
            total = jnp.dot(hid[g, 0], wd[0, :, part], preferred_element_type=jnp.float32)
            total += jnp.dot(hid[g, 1], wd[1, :, part], preferred_element_type=jnp.float32)
            for ref, piece in ((first_to, total[:many]), (second_to, total[many:])):
                ref[:, :, part] = piece.reshape(span, rows, wide).astype(ref.dtype)
            return 0

        lax.fori_loop(0, half // wide, step, 0)

    low = z < span // 2
    arrivals = [flipped(z, 1), jnp.where(low, 2, 1), jnp.where(low, 3, 0)]
    inner = (z > 0) & (z < span - 1)

    def passed_on(j):
        i = arrivals[j]
        return row_copy(i, jnp.where(i < z, upper, lower), 2 + j)

    def gathered(i):
        start(by_x(i))
        start(by_y(i))
        start(to_core[0](i))

    def crossed(i):
        by_x(i).wait_recv()
        start(far_left(i))
        start(to_core[1](i))
        by_y(i).wait_recv()
        start(far_right(i))
        start(to_core[2](i))

    def cornered(i):
        far_left(i).wait_recv()
        start(core_left(i))
        far_right(i).wait_recv()
        start(core_right(i))

    loads[0].wait()
    pl.semaphore_wait(barrier, len(partners))
    pl.when(z < span - 1)(lambda: row_copy(z, upper, 0).start())
    pl.when(z > 0)(lambda: row_copy(z, lower, 1).start())
    gathered(z)
    start(swap_down)
    done = [z]
    for j, i in enumerate(arrivals):
        row_copy(i, upper, 2 + j).wait_recv()
        pl.when(inner)(lambda j=j: passed_on(j).start())
        gathered(i)
        crossed(done[-1])
        if len(done) > 1:
            cornered(done[-2])
        done.append(i)
    for load in loads[1:3]:
        load.wait()
    for i in range(span):
        to_core[0](i).wait_recv()
    project(0)
    crossed(done[-1])
    cornered(done[-2])
    for i in range(span):
        to_core[1](i).wait_recv()
    project(1)
    cornered(done[-1])
    for i in range(span):
        to_core[2](i).wait_recv()
    project(2)
    loads[3].wait()
    swap_down.wait_recv()
    expand(1, x_out.at[0], x_pend)
    expand(2, y_pend, y_out.at[1])
    order = [(p, (z + p) % span) for p in (2, 3, 1, 0)]
    ahead = 2
    for _, i in order[:ahead]:
        start(x_early(i))
        start(y_early(i))
    for i in range(span):
        core_left(i).wait_recv()
        core_right(i).wait_recv()
    project(3)
    expand(0, own_sum.at[0], own_sum.at[1])
    expand(3, d_out.at[0], d_out.at[1])
    for _, i in order[:ahead]:
        start(d_to_x(i))
        start(d_to_y(i))

    def finish(p, i):
        for copy in (x_early(i), y_early(i), x_late(i), y_late(i)):
            copy.wait_recv()
        for r in range(2):
            total = own_sum[r, i] + x_in[r, i].astype(jnp.float32) + y_in[r, i].astype(jnp.float32)
            if (r, p) == (0, 0):
                own_sum[r, i] = total
            else:
                z_out[r, p] = total.astype(jnp.bfloat16)
                start(home[r, p])

    for n, (p, i) in enumerate(order):
        d_to_y(i).wait_recv()
        x_out[1, i] = (x_pend[i] + d_in[1, i].astype(jnp.float32)).astype(jnp.bfloat16)
        start(x_late(i))
        d_to_x(i).wait_recv()
        y_out[0, i] = (y_pend[i] + d_in[0, i].astype(jnp.float32)).astype(jnp.bfloat16)
        start(y_late(i))
        if n + ahead < span:
            start(x_early(order[n + ahead][1]))
            start(y_early(order[n + ahead][1]))
            start(d_to_x(order[n + ahead][1]))
            start(d_to_y(order[n + ahead][1]))
        if n:
            finish(*order[n - 1])
    finish(*order[-1])
    for copy in home.values():
        copy.wait_recv()
    total = own_sum[0, z]
    for p in range(1, span):
        total += z_in[0, p].astype(jnp.float32)
    out_ref[:, my_half] = total.astype(jnp.bfloat16)
    total = z_in[1, 0].astype(jnp.float32)
    for p in range(1, span):
        total += z_in[1, p].astype(jnp.float32)
    out_ref[:, other_half] = total.astype(jnp.bfloat16)
    for copy in sent:
        copy.wait_send()
    pl.when(z < span - 1)(lambda: row_copy(z, upper, 0).wait_send())
    pl.when(z > 0)(lambda: row_copy(z, lower, 1).wait_send())
    for j in range(span - 1):
        pl.when(inner)(lambda j=j: passed_on(j).wait_send())


def squares(tokens, slot_ids, route_weights, pair_swap, w_gate, w_up, w_down):
    span = lax.axis_size("expert") // SQUARE_SLOTS
    rows, width = tokens.shape
    hidden = w_gate.shape[2]
    half = width // 2
    wide = width + LANES
    group = 2 * span * rows
    messages = 9 * span + 1 + 4 + 6 * span + 2 * span + 4 + span
    bf16, f32 = jnp.bfloat16, jnp.float32
    column = (span, rows, half)
    vmem = pl.BlockSpec(memory_space=pltpu.VMEM)
    hbm = pl.BlockSpec(memory_space=pl.ANY)
    return pl.pallas_call(
        functools.partial(kernel, span),
        out_shape=jax.ShapeDtypeStruct((rows, width), bf16),
        in_specs=[pl.BlockSpec(memory_space=pltpu.SMEM), vmem, vmem, hbm, hbm, hbm, hbm],
        out_specs=vmem,
        scratch_shapes=[
            pltpu.VMEM((4, 2, span, rows, wide), bf16),
            pltpu.VMEM((width, hidden), bf16),
            pltpu.VMEM((width, hidden), bf16),
            pltpu.VMEM((2, hidden, half), bf16),
            pltpu.VMEM((group, hidden), f32),
            pltpu.VMEM((group, hidden), f32),
            pltpu.VMEM((4, 2, group, hidden), bf16),
            pltpu.VMEM((4, group, hidden), bf16),
            pltpu.VMEM((2,) + column, f32),
            pltpu.VMEM(column, f32),
            pltpu.VMEM(column, f32),
        ]
        + [pltpu.VMEM((2,) + column, bf16)] * 8
        + [
            pltpu.SemaphoreType.DMA((4,)),
            pltpu.SemaphoreType.DMA((messages,)),
            pltpu.SemaphoreType.DMA((messages,)),
            pltpu.SemaphoreType.DMA((span + 1,)),
            pltpu.SemaphoreType.DMA((span,)),
        ],
        compiler_params=pltpu.CompilerParams(
            collective_id=0, has_side_effects=True, vmem_limit_bytes=56 * 2**20
        ),
    )(pair_swap, slot_ids.T, route_weights.T, tokens, w_gate, w_up, w_down)


def whole(tokens, slot_ids, route_weights, pair_swap, w_gate, w_up, w_down):
    slots = 2 * pair_swap.shape[0]
    own = lax.axis_index("expert") % slots
    pair = jnp.arange(pair_swap.shape[0], dtype=jnp.int32)
    swap = jnp.sum(jnp.where(pair == own // 2, pair_swap, 0))
    slot = own + swap * (1 - 2 * (own % 2))
    named = slot_ids[:, :, None] == jnp.arange(slots, dtype=jnp.int32)
    dense = jnp.sum(jnp.where(named, route_weights[:, :, None], 0.0), 1)
    rows = lax.all_gather(tokens, "expert", axis=0, tiled=True)
    dense = lax.all_gather(dense, "expert", axis=0, tiled=True)
    mine = jnp.arange(slots, dtype=jnp.int32) == slot
    weight = jnp.sum(jnp.where(mine, dense, 0.0), 1, keepdims=True)
    gate = jnp.dot(rows, w_gate[0], preferred_element_type=jnp.float32)
    up = jnp.dot(rows, w_up[0], preferred_element_type=jnp.float32)
    hidden = (jax.nn.silu(gate) * up).astype(jnp.bfloat16)
    value = jnp.dot(hidden, w_down[0], preferred_element_type=jnp.float32) * weight
    mixed = lax.psum_scatter(value, "expert", scatter_dimension=0, tiled=True)
    return mixed.astype(jnp.bfloat16)


def on_device(*args):
    slots = 2 * args[3].shape[0]
    square = slots == SQUARE_SLOTS and lax.axis_size("expert") == SQUARE_SLOTS * COLUMN
    return (squares if square else whole)(*args)


def solution(mesh):
    return jax.shard_map(
        on_device,
        mesh=mesh,
        in_specs=(
            P(("dp", "expert"), None),
            P(("dp", "expert"), None),
            P(("dp", "expert"), None),
            P(),
            P("expert", None, None),
            P("expert", None, None),
            P("expert", None, None),
        ),
        out_specs=P(("dp", "expert"), None),
        check_vma=False,
    )
```
